256 devices in a mesh: row: 16 (over z_hi, y), col: 16 (over x, z_lo, core).
Axes of the slice: x: 4, y: 4, z: 8 (z_hi: 4, z_lo: 2; z = z_hi * 2 + z_lo), core: 2. Of those that a mesh axis runs over, the one named last changes fastest.
Arguments:
- spectra: bfloat16 [8, 2, 512, 8192], P(None, None, 'col', 'row'), may hold values from -400 to 400, as said below
- channel_mask: int32 [8192], P('row'), may hold values 0 or 1
- pairing: int32 [16, 16], P('row'), may hold values from 0 to 15, each once within a row
Outputs:
- correlations: bfloat16 [256, 256, 8192], P('col', None, 'row')
The draws below stay inside these ranges and needn't reach their ends.
Inputs may be any that keep to these rules, and one draw needn't show every extreme that they name: Each row of pairing names every block once. `spectra`: finite values of varying scale per segment, channel and frequency.
All inputs are finite; a program needn't handle non-finite values. No bound on the sum of `channel_mask` on one device may be relied on, other than what follows from the above.
Results may differ from the reference program's by a relative error of at most 0.0068.
Values may be sent and summed in bfloat16 or wider, within the bound.
No kernel may reach another device: no remote copies, remote signals or barrier semaphores. Data moves between devices by JAX's collectives and lax.ppermute only.
A program may use at most 128 MiB of HBM per device.

```python
import math
import jax
import jax.numpy as jnp
from jax import lax

BLOCK = 512
FREQ = 512
LAGS = 256
SEG = 8
SOURCES = 16
NB = 16
CH = 8192


def draw_spectra(key, part):
    key = jax.random.fold_in(key, 11)
    key_base, key_freq, key_chan = jax.random.split(key, 3)
    freq_index = jnp.arange(FREQ).astype(jnp.float32)
    ramp_scale = 1.0 + 2.0 * freq_index / (FREQ - 1)
    freq_scale = ramp_scale * jnp.exp(jax.random.uniform(key_freq, (FREQ,), jnp.float32, math.log(0.7), math.log(1.4)))
    base = jax.random.normal(key_base, (SEG, 2, FREQ, CH), jnp.float32)
    base = jnp.clip(base, -6.0, 6.0)
    chan_scale = jnp.exp(jax.random.uniform(key_chan, (SEG, 1, 1, CH), jnp.float32, 0.0, math.log(10.0)))
    values = base * chan_scale * freq_scale[None, None, :, None]
    return values.astype(jnp.bfloat16)


def plant(result, stream_key, smallest, largest):
    extent = result.shape
    spot = [jax.random.randint(jax.random.fold_in(stream_key, axis), (), 0, extent[axis]) for axis in range(len(extent))]
    result = result.at[tuple(spot)].set(smallest)
    longest = extent.index(max(extent))
    spot[longest] = (spot[longest] + 1) % extent[longest]
    return result.at[tuple(spot)].set(largest)


def setup_inputs(seed: int = 0) -> dict:
    arg_keys = jax.random.split(jax.random.key(seed), 4)
    spectra = draw_spectra(jax.random.fold_in(arg_keys[3], 71), 0)
    channel_mask = plant((jax.random.randint(arg_keys[1], (CH,), 0, 8) < 7).astype(jnp.int32), jax.random.fold_in(arg_keys[1], 1), 0, 1)
    pairing = jax.vmap(lambda own: jax.random.permutation(own, NB))(jax.random.split(arg_keys[2], NB)).reshape((NB, NB)).astype(jnp.int32)
    return dict(spectra=spectra, channel_mask=channel_mask, pairing=pairing)


def lag_kernel():
    lag_index = jnp.arange(LAGS, dtype=jnp.int32)
    freq_index = jnp.arange(FREQ, dtype=jnp.int32)
    phase_step = lag_index[:, None] * freq_index[None, :] % (2 * FREQ)
    angles = phase_step.astype(jnp.float32) * (math.pi / FREQ)
    weights = jnp.where(freq_index == 0, 0.5, 1.0).astype(jnp.float32) / math.sqrt(2.0 * FREQ)
    table = jnp.stack([weights[None, :] * jnp.cos(angles), -weights[None, :] * jnp.sin(angles)], axis=1)
    return table.astype(jnp.bfloat16)

def reference(spectra, channel_mask, pairing):
    masked = spectra.astype(jnp.float32) * channel_mask.astype(jnp.float32)[None, None, None, :]
    energy = lax.optimization_barrier(jnp.sum(masked * masked, axis=(1, 2))) / FREQ
    whitened = (masked / jnp.sqrt(energy + 1e-06)[:, None, None, :]).astype(jnp.bfloat16)
    blocks = whitened.reshape(SEG, 2, FREQ, NB, BLOCK)
    sources = blocks[..., ::BLOCK // SOURCES]
    table = lag_kernel().astype(jnp.float32)

    def per_block(block_id):
        receiver = lax.dynamic_slice_in_dim(whitened, (block_id * BLOCK).astype(jnp.int32), BLOCK, 3).astype(jnp.float32)
        chosen = jnp.take(sources, pairing[block_id], axis=3).reshape(SEG, 2, FREQ, NB * SOURCES).astype(jnp.float32)
        rotated = jnp.stack([-receiver[:, 1], receiver[:, 0]], axis=1)
        real_part = jnp.einsum('skfn,skfb->nfb', chosen, receiver)
        imag_part = jnp.einsum('skfn,skfb->nfb', chosen, rotated)
        cross = jnp.stack([real_part, imag_part], axis=1).astype(jnp.bfloat16)
        lagged = jnp.einsum('tkf,nkfb->ntb', table, cross.astype(jnp.float32))
        return lagged.astype(jnp.bfloat16)
    stacked = lax.map(per_block, jnp.arange(NB, dtype=jnp.int32))
    return jnp.transpose(stacked, (1, 2, 0, 3)).reshape(NB * SOURCES, LAGS, NB * BLOCK)
```

```python
import math

import jax
import jax.numpy as jnp
import numpy as np
from jax import lax
from jax.experimental import pallas as pl
from jax.experimental.pallas import tpu as pltpu
from jax.sharding import PartitionSpec as P

BLOCK = 512
FREQ = 512
LAGS = 256
SEG = 8
SOURCES = 16
HALF = 16
STEP = BLOCK // SOURCES
GROUP = 2 * SEG * HALF
EPS = 1e-06
MIB = 1 << 20

BATCHES = (
    (
        ((0, 0, 0), (0, 0, 1)),
        ((1, 0, 0), (1, 0, 1)),
        ((3, 0, 0), (3, 0, 1)),
        ((0, 1, 0), (0, 1, 1)),
    ),
    (
        ((2, 0, 0), (1, 1, 1)),
        ((3, 1, 0), (2, 0, 1)),
        ((1, 1, 0), (3, 1, 1)),
    ),
    (
        ((2, 1, 0),),
        ((2, 1, 1),),
    ),
)


def ordered_groups(batch):
    return [(dx, dz, dc, half) for piece in batch for dc in (0, 1) for dx, dz, half in piece]


GROUPS = [group for batch in BATCHES for group in ordered_groups(batch)]


def dot(a, b, dims=((1,), (0,))):
    return lax.dot_general(a, b, (dims, ((), ())), preferred_element_type=jnp.float32)


def prepare_kernel(x_ref, mask_ref, out_ref):
    mask = mask_ref[...].astype(jnp.float32)
    row = lax.broadcasted_iota(jnp.int32, (SOURCES, BLOCK), 0)
    col = lax.broadcasted_iota(jnp.int32, (SOURCES, BLOCK), 1)
    pick = jnp.where(col == row * STEP, jnp.broadcast_to(mask, (SOURCES, BLOCK)), 0.0).astype(jnp.bfloat16)
    for half in range(2):
        part = x_ref[:, :, half * HALF : (half + 1) * HALF, :].reshape(GROUP, BLOCK)
        out_ref[0, :, half * GROUP : (half + 1) * GROUP] = dot(pick, part, ((1,), (1,))).astype(jnp.bfloat16)
    sums = []
    for seg in range(SEG):
        value = x_ref[seg].astype(jnp.float32).reshape(4 * HALF, BLOCK)
        sums.append(jnp.sum(value * value, axis=0, keepdims=True))
    energy = jnp.concatenate(sums, axis=0) * mask
    high = energy.astype(jnp.bfloat16).astype(jnp.float32)
    out_ref[1] = jnp.concatenate([high, energy - high], axis=0).astype(jnp.bfloat16)


def prepare(x, mask):
    return pl.pallas_call(
        prepare_kernel,
        out_shape=jax.ShapeDtypeStruct((2, SOURCES, BLOCK), jnp.bfloat16),
        compiler_params=pltpu.CompilerParams(vmem_limit_bytes=16 * MIB),
    )(x, mask)


def choose_kernel(index_ref, gathered_ref, out_ref):
    for slot in range(16):
        out_ref[slot] = gathered_ref[index_ref[slot]]


def choose(index, gathered):
    return pl.pallas_call(
        choose_kernel,
        out_shape=jax.ShapeDtypeStruct(gathered.shape, gathered.dtype),
        in_specs=[pl.BlockSpec(memory_space=pltpu.SMEM), pl.BlockSpec(memory_space=pltpu.VMEM)],
        compiler_params=pltpu.CompilerParams(vmem_limit_bytes=16 * MIB),
    )(index, gathered)


def scales_kernel(src_ref, energy_ref, mask_ref, scale_ref, white_ref):
    energy = jnp.zeros((SEG, BLOCK), jnp.float32)
    for n in range(16):
        both = energy_ref[n].astype(jnp.float32)
        energy = energy + (both[:SEG] + both[SEG:])
    mask = mask_ref[...].astype(jnp.float32)
    scale_ref[...] = mask * lax.rsqrt(energy / FREQ + EPS)

    power = jnp.zeros((SOURCES, 2 * GROUP), jnp.float32)
    for n in range(16):
        value = src_ref[n].astype(jnp.float32)
        power = power + value * value
    power = power[:, :GROUP] + power[:, GROUP:]
    row = lax.broadcasted_iota(jnp.int32, (GROUP, GROUP), 0)
    col = lax.broadcasted_iota(jnp.int32, (GROUP, GROUP), 1)
    same = jnp.where(row // (2 * HALF) == col // (2 * HALF), 1.0, 0.0)
    total = lax.dot_general(
        power, same, (((1,), (0,)), ((), ())), precision=lax.Precision.HIGHEST, preferred_element_type=jnp.float32
    )
    factor = lax.rsqrt(total / FREQ + EPS)
    turn = jnp.where(row == col + HALF, 1.0, 0.0) - jnp.where(row == col - HALF, 1.0, 0.0)
    first = (col // HALF) % 2 == 0
    turn = jnp.where(first, jnp.maximum(turn, 0.0), jnp.minimum(turn, 0.0)).astype(jnp.bfloat16)
    for g, (dx, dz, dc, half) in enumerate(GROUPS):
        n = (dc * 2 + dz) * 4 + dx
        value = src_ref[n, :, half * GROUP : (half + 1) * GROUP].astype(jnp.float32)
        real = (value * factor).astype(jnp.bfloat16)
        white_ref[g, :SOURCES] = real
        white_ref[g, SOURCES:] = dot(real, turn).astype(jnp.bfloat16)


def scales(src, energy, mask):
    return pl.pallas_call(
        scales_kernel,
        out_shape=(
            jax.ShapeDtypeStruct((SEG, BLOCK), jnp.float32),
            jax.ShapeDtypeStruct((len(GROUPS), 2 * SOURCES, GROUP), jnp.bfloat16),
        ),
        compiler_params=pltpu.CompilerParams(vmem_limit_bytes=16 * MIB),
    )(src, energy, mask)


def cross_kernel(count, first_group, halves, *refs):
    pieces, scale_ref, white_ref, out_ref, held = refs[:count], *refs[count:]
    for n, piece in enumerate(pieces):

        def whiten(seg, carry, n=n, piece=piece):
            factor = scale_ref[pl.ds(seg, 1), :].reshape(1, 1, BLOCK)
            value = (piece[seg].astype(jnp.float32) * factor).astype(jnp.bfloat16)
            for half in range(halves):
                part = value[:, half * HALF : (half + 1) * HALF, :].reshape(2 * HALF, BLOCK)
                held[n * halves + half, pl.ds(pl.multiple_of(seg * 2 * HALF, 2 * HALF), 2 * HALF), :] = part
            return carry

        lax.fori_loop(0, SEG, whiten, 0)

    lane = lax.broadcasted_iota(jnp.int32, (HALF, GROUP), 1)
    sub = lax.broadcasted_iota(jnp.int32, (HALF, GROUP), 0)
    diagonal = lane % HALF == sub

    def group(g, carry):
        white = white_ref[first_group + g].astype(jnp.float32)
        right = held[g]
        for quad in range(4):
            rows = []
            for v in range(quad * 4, quad * 4 + 4):
                for part in range(2):
                    one = white[part * SOURCES + v : part * SOURCES + v + 1, :]
                    rows.append(jnp.where(diagonal, jnp.broadcast_to(one, (HALF, GROUP)), 0.0))
            left = jnp.concatenate(rows, axis=0).astype(jnp.bfloat16)
            value = dot(left, right).astype(jnp.bfloat16).reshape(4, 2 * HALF, BLOCK)
            out_ref[quad * 4 : quad * 4 + 4, pl.ds(pl.multiple_of(g * 2 * HALF, 2 * HALF), 2 * HALF), :] = value
        return carry

    lax.fori_loop(0, count * halves, group, 0)


def cross(pieces, scale, white, first_group):
    halves = pieces[0].shape[2] // HALF
    groups = len(pieces) * halves

    def kernel(*refs):
        cross_kernel(len(pieces), first_group, halves, *refs)

    return pl.pallas_call(
        kernel,
        out_shape=jax.ShapeDtypeStruct((SOURCES, groups * 2 * HALF, BLOCK), jnp.bfloat16),
        scratch_shapes=[pltpu.VMEM((groups, GROUP, BLOCK), jnp.bfloat16)],
        compiler_params=pltpu.CompilerParams(vmem_limit_bytes=40 * MIB),
        cost_estimate=pl.CostEstimate(
            flops=groups * 2 * 512 * 256 * 512, bytes_accessed=groups * 512 * 1024, transcendentals=0
        ),
    )(*pieces, scale, white)


def lag_kernel(table_ref, *refs):
    *cross_refs, out_ref = refs
    total, start = None, 0
    for ref in cross_refs:
        rows = ref.shape[1]
        term = dot(table_ref[:, start : start + rows], ref[0])
        total = term if total is None else total + term
        start += rows
    out_ref[0] = total.astype(jnp.bfloat16)


def lag(table, parts):
    return pl.pallas_call(
        lag_kernel,
        grid=(SOURCES,),
        out_shape=jax.ShapeDtypeStruct((SOURCES, LAGS, BLOCK), jnp.bfloat16),
        in_specs=[pl.BlockSpec((LAGS, 2 * FREQ), lambda v: (0, 0))]
        + [pl.BlockSpec((1, part.shape[1], BLOCK), lambda v: (v, 0, 0)) for part in parts],
        out_specs=pl.BlockSpec((1, LAGS, BLOCK), lambda v: (v, 0, 0)),
        compiler_params=pltpu.CompilerParams(vmem_limit_bytes=32 * MIB),
    )(table, *parts)


def lag_table(ix, iz, ic):
    dx, dz, dc, half = (np.array([g[i] for g in GROUPS], np.int32) for i in range(4))
    spread = lambda a: np.repeat(a, 2 * HALF)
    part = np.tile(np.repeat(np.arange(2, dtype=np.int32), HALF), len(GROUPS))
    inner = np.tile(np.arange(HALF, dtype=np.int32), 2 * len(GROUPS)) + HALF * spread(half)
    place = ((ix + 4 - spread(dx)) % 4) * 4 + (iz ^ spread(dz)) * 2 + (ic ^ spread(dc))
    freq = (place * 2 * HALF + inner)[None, :]
    time = lax.broadcasted_iota(jnp.int32, (LAGS, 2 * FREQ), 0)
    phase = (time * freq + part[None, :] * (FREQ // 2)) % (2 * FREQ)
    weight = jnp.where(freq == 0, 0.5, 1.0).astype(jnp.float32) / math.sqrt(2.0 * FREQ)
    return (weight * jnp.cos(phase.astype(jnp.float32) * (math.pi / FREQ))).astype(jnp.bfloat16)


def send(value, axis, where):
    return lax.ppermute(value, axis, [(n, where(n)) for n in range(16)])


def on_slow(n, d):
    return (n // 4 + d) % 4 * 4 + n % 4


def on_fast(n, d):
    return n // 4 * 4 + (n % 4 + d) % 4


def on_device(x, mask, pairing):
    row, col = lax.axis_index("row"), lax.axis_index("col")
    iz_hi, iy = row // 4, row % 4
    ix, iz, ic = col // 4, col // 2 % 2, col % 2
    up = lambda v: send(v, "col", lambda n: on_slow(n, 1))
    down = lambda v: send(v, "col", lambda n: on_slow(n, -1))
    across = lambda v: send(v, "col", lambda n: n ^ 2)
    sibling = lambda v: send(v, "col", lambda n: n ^ 1)
    low = lambda v: v[:, :, :HALF]
    high = lambda v: v[:, :, HALF:]
    join = lambda a, b: jnp.concatenate([a, b], axis=2)

    a1, b1, c1 = up(x), down(x), across(x)
    a2 = up(join(low(a1), high(c1)))
    b2 = down(join(low(c1), high(b1)))
    c2 = across(join(low(a1), high(b1)))
    a3 = up(high(a2))
    b3 = down(low(b2))

    mask_row = mask.reshape(1, BLOCK)
    prepared = prepare(x, mask_row)
    own, partial = prepared[:1], prepared[1:]
    by_y = jnp.concatenate([own] + [send(own, "row", lambda n, d=d: on_fast(n, d)) for d in (1, 2, 3)])
    by_row = jnp.concatenate([by_y] + [send(by_y, "row", lambda n, d=d: on_slow(n, d)) for d in (1, 2, 3)])
    slot = np.arange(16, dtype=np.int32)
    target = (ix + slot // 4) % 4 * 4 + (iz ^ (slot // 2 % 2)) * 2 + (ic ^ (slot % 2))
    block = pairing[0][target]
    index = (iz_hi + 4 - block // 4) % 4 * 4 + (iy + 4 - block % 4) % 4
    chosen = choose(index, by_row).reshape(4, 2, 2, SOURCES, BLOCK)

    def flat(parts):
        return jnp.concatenate([part.reshape(-1, SOURCES, BLOCK) for part in parts])

    got = [flat([chosen[0], partial])]
    got += [send(flat([chosen[d], partial]), "col", lambda n, d=d: on_slow(n, d)) for d in (1, 2, 3)]
    got = jnp.stack(got)
    src, energy = got[:, :4].reshape(4, 2, 2, SOURCES, BLOCK), got[:, 4]
    other = across(flat([src[:, 1], energy]))
    src = jnp.stack([src[:, 0], other[:8].reshape(4, 2, SOURCES, BLOCK)])
    energy = jnp.stack([energy, other[8:]])
    other = sibling(flat([src[:, :, 1], energy]))
    src = flat([src[:, :, 0], other[:8]])
    energy = flat([energy, other[8:]])
    scale, white = scales(src, energy, mask_row)

    table = lag_table(ix, iz, ic)
    parts, first = [], 0
    for batch, pieces in zip(BATCHES, ((x, a1, b1, c1), (a2, b2, c2), (b3, a3)), strict=True):
        both = [piece for mine in pieces for piece in (mine, sibling(mine))]
        parts.append(cross(both, scale, white, first))
        first += len(ordered_groups(batch))
    return lag(table, parts)


def solution(mesh):
    in_specs = (P(None, None, "col", "row"), P("row"), P("row", None))
    out_specs = P("col", None, "row")
    return jax.shard_map(on_device, mesh=mesh, in_specs=in_specs, out_specs=out_specs, check_vma=False)
```

```python
import math

import jax
import jax.numpy as jnp
import numpy as np
from jax import lax
from jax.experimental import pallas as pl
from jax.experimental.pallas import tpu as pltpu
from jax.sharding import PartitionSpec as P

BLOCK = 512
FREQ = 512
LAGS = 256
SEG = 8
SOURCES = 16
HALF = 16
STEP = BLOCK // SOURCES
GROUP = 2 * SEG * HALF
EPS = 1e-06
MIB = 1 << 20

BATCHES = (
    (
        ((0, 0, 0), (0, 0, 1)),
        ((1, 0, 0), (1, 0, 1)),
        ((3, 0, 0), (3, 0, 1)),
        ((0, 1, 0), (0, 1, 1)),
    ),
    (
        ((2, 0, 0), (1, 1, 1)),
        ((3, 1, 0), (2, 0, 1)),
        ((1, 1, 0), (3, 1, 1)),
    ),
    (((2, 1, 1),), ((2, 1, 0),)),
)


def ordered_groups(batch):
    return [(dx, dz, dc, half) for piece in batch for dc in (0, 1) for dx, dz, half in piece]


GROUPS = [group for batch in BATCHES for group in ordered_groups(batch)]

EARLY = sum(len(ordered_groups(batch)) for batch in BATCHES[:2])


def dot(a, b, dims=((1,), (0,))):
    return lax.dot_general(a, b, (dims, ((), ())), preferred_element_type=jnp.float32)


def place(col, dx, dz, dc):
    x, z, core = col // 4, col // 2 % 2, col % 2
    return (x + 4 - dx) % 4 * 4 + (z + dz) % 2 * 2 + (core + dc) % 2


def prepare_kernel(x_ref, mask_ref, src_ref, energy_ref, good_ref):
    mask = mask_ref[...].astype(jnp.float32)
    good_ref[...] = mask
    row = lax.broadcasted_iota(jnp.int32, (SOURCES, BLOCK), 0)
    col = lax.broadcasted_iota(jnp.int32, (SOURCES, BLOCK), 1)
    pick = jnp.where(col == row * STEP, jnp.broadcast_to(mask, (SOURCES, BLOCK)), 0.0).astype(jnp.bfloat16)
    for half in range(2):
        part = x_ref[:, :, half * HALF : (half + 1) * HALF, :].reshape(GROUP, BLOCK)
        src_ref[:, half * GROUP : (half + 1) * GROUP] = dot(pick, part, ((1,), (1,))).astype(jnp.bfloat16)
    sums = []
    for seg in range(SEG):
        value = x_ref[seg].astype(jnp.float32).reshape(4 * HALF, BLOCK)
        sums.append(jnp.sum(value * value, axis=0, keepdims=True))
    energy = jnp.concatenate(sums, axis=0) * mask
    high = energy.astype(jnp.bfloat16).astype(jnp.float32)
    energy_ref[...] = jnp.concatenate([high, energy - high], axis=0).astype(jnp.bfloat16)


def prepare(x, mask):
    return pl.pallas_call(
        prepare_kernel,
        out_shape=(jax.ShapeDtypeStruct((SOURCES, BLOCK), jnp.bfloat16),) * 2
        + (jax.ShapeDtypeStruct((1, BLOCK), jnp.float32),),
        compiler_params=pltpu.CompilerParams(vmem_limit_bytes=16 * MIB),
    )(x, mask)


def choose_kernel(row_ref, pairing_ref, gathered_ref, energy_ref, out_ref):
    row = row_ref[0]
    for slot in range(16):
        block = pairing_ref[0, slot]
        out_ref[slot, :SOURCES] = gathered_ref[block % 4, (row // 4 + 4 - block // 4) % 4]
        out_ref[slot, SOURCES:] = energy_ref[...]


def choose(row, pairing, gathered, energy):
    return pl.pallas_call(
        choose_kernel,
        out_shape=jax.ShapeDtypeStruct((16, 2 * SOURCES, BLOCK), jnp.bfloat16),
        in_specs=[pl.BlockSpec(memory_space=pltpu.SMEM)] * 2 + [pl.BlockSpec(memory_space=pltpu.VMEM)] * 2,
        compiler_params=pltpu.CompilerParams(vmem_limit_bytes=8 * MIB),
    )(row, pairing, gathered, energy)


def scales_kernel(col_ref, got_ref, good_ref, scale_ref, white_ref):
    energy = jnp.zeros((SEG, BLOCK), jnp.float32)
    for n in range(16):
        both = got_ref[n, SOURCES:].astype(jnp.float32)
        energy = energy + (both[:SEG] + both[SEG:])
    scale_ref[...] = good_ref[...] * lax.rsqrt(energy / FREQ + EPS)

    power = jnp.zeros((SOURCES, 2 * GROUP), jnp.float32)
    for n in range(16):
        value = got_ref[n, :SOURCES].astype(jnp.float32)
        power = power + value * value
    power = power[:, :GROUP] + power[:, GROUP:]
    row = lax.broadcasted_iota(jnp.int32, (GROUP, GROUP), 0)
    col = lax.broadcasted_iota(jnp.int32, (GROUP, GROUP), 1)
    same = jnp.where(row // (2 * HALF) == col // (2 * HALF), 1.0, 0.0)
    total = lax.dot_general(
        power, same, (((1,), (0,)), ((), ())), precision=lax.Precision.HIGHEST, preferred_element_type=jnp.float32
    )
    factor = lax.rsqrt(total / FREQ + EPS)
    turn = jnp.where(row == col + HALF, 1.0, 0.0) - jnp.where(row == col - HALF, 1.0, 0.0)
    first = (col // HALF) % 2 == 0
    turn = jnp.where(first, jnp.maximum(turn, 0.0), jnp.minimum(turn, 0.0)).astype(jnp.bfloat16)
    for g, (dx, dz, dc, half) in enumerate(GROUPS):
        n = place(col_ref[0], dx, dz, dc)
        value = got_ref[n, :SOURCES, half * GROUP : (half + 1) * GROUP].astype(jnp.float32)
        real = (value * factor).astype(jnp.bfloat16)
        white_ref[g, :SOURCES] = real
        white_ref[g, SOURCES:] = dot(real, turn).astype(jnp.bfloat16)


def scales(col, got, good):
    return pl.pallas_call(
        scales_kernel,
        out_shape=(
            jax.ShapeDtypeStruct((SEG, BLOCK), jnp.float32),
            jax.ShapeDtypeStruct((len(GROUPS), 2 * SOURCES, GROUP), jnp.bfloat16),
        ),
        in_specs=[pl.BlockSpec(memory_space=pltpu.SMEM)] + [pl.BlockSpec(memory_space=pltpu.VMEM)] * 2,
        compiler_params=pltpu.CompilerParams(vmem_limit_bytes=8 * MIB),
    )(col, got, good)


def cross_groups(pieces, first_group, scale_ref, white_ref, crossed, raw, right0, right1, left0, left1, sems):
    copies = []
    for piece in pieces:
        for half in range(piece.shape[2] // HALF):
            g = len(copies)
            copies.append(pltpu.make_async_copy(piece.at[:, :, pl.ds(half * HALF, HALF), :], raw.at[g], sems.at[g]))
    for copy in copies:
        copy.start()
    groups = len(copies)

    def arrive(g):
        pltpu.make_async_copy(raw.at[g], raw.at[g], sems.at[g]).wait()

    lane = lax.broadcasted_iota(jnp.int32, (HALF, GROUP), 1)
    sub = lax.broadcasted_iota(jnp.int32, (HALF, GROUP), 0)
    diagonal = lane % HALF == sub

    def ready(g, right, left):
        for seg in range(SEG):
            value = raw[g, seg].astype(jnp.float32) * scale_ref[seg : seg + 1, :].reshape(1, 1, BLOCK)
            right[seg * 2 * HALF : (seg + 1) * 2 * HALF, :] = value.astype(jnp.bfloat16).reshape(2 * HALF, BLOCK)
        white = white_ref[first_group + g].astype(jnp.float32)
        for v in range(SOURCES):
            for part in range(2):
                one = white[part * SOURCES + v : part * SOURCES + v + 1, :]
                tile = jnp.where(diagonal, jnp.broadcast_to(one, (HALF, GROUP)), 0.0).astype(jnp.bfloat16)
                left[(2 * v + part) * HALF : (2 * v + part + 1) * HALF, :] = tile

    def multiply(g, right, left):
        rows = pl.ds(pl.multiple_of(g * 2 * HALF, 2 * HALF), 2 * HALF)
        for n in range(0, BLOCK, GROUP):
            value = dot(left[...], right[:, n : n + GROUP]).astype(jnp.bfloat16)
            crossed[:, rows, n : n + GROUP] = value.reshape(SOURCES, 2 * HALF, GROUP)

    arrive(0)
    ready(0, right0, left0)

    def pair(i, carry):
        g = 2 * i
        arrive(g + 1)
        multiply(g, right0, left0)
        ready(g + 1, right1, left1)

        @pl.when(i < groups // 2 - 1)
        def _():
            arrive(g + 2)

        multiply(g + 1, right1, left1)
        ready(jnp.minimum(g + 2, groups - 1), right0, left0)
        return carry

    lax.fori_loop(0, groups // 2, pair, 0)


def cross_scratch(groups):
    return [
        pltpu.VMEM((groups, SEG, 2, HALF, BLOCK), jnp.bfloat16),
        pltpu.VMEM((GROUP, BLOCK), jnp.bfloat16),
        pltpu.VMEM((GROUP, BLOCK), jnp.bfloat16),
        pltpu.VMEM((2 * SOURCES * HALF, GROUP), jnp.bfloat16),
        pltpu.VMEM((2 * SOURCES * HALF, GROUP), jnp.bfloat16),
        pltpu.SemaphoreType.DMA((groups,)),
    ]


def cross(pieces, scale, white):
    def kernel(*refs):
        scale_ref, white_ref, out_ref = refs[len(pieces) : len(pieces) + 3]
        cross_groups(refs[: len(pieces)], 0, scale_ref, white_ref, out_ref, *refs[len(pieces) + 3 :])

    return pl.pallas_call(
        kernel,
        out_shape=jax.ShapeDtypeStruct((SOURCES, EARLY * 2 * HALF, BLOCK), jnp.bfloat16),
        in_specs=[pl.BlockSpec(memory_space=pl.ANY)] * len(pieces) + [pl.BlockSpec(memory_space=pltpu.VMEM)] * 2,
        scratch_shapes=cross_scratch(EARLY),
        compiler_params=pltpu.CompilerParams(vmem_limit_bytes=28 * MIB),
        cost_estimate=pl.CostEstimate(flops=10**9, bytes_accessed=MIB, transcendentals=0),
    )(*pieces, scale, white)


def finish(pieces, early, scale, white, table):
    count, late = len(pieces), len(GROUPS) - EARLY

    def kernel(*refs):
        early_ref, scale_ref, white_ref, table_ref, out_ref, crossed, staged0, staged1, out_sems = refs[count : count + 9]
        cross_groups(refs[:count], EARLY, scale_ref, white_ref, crossed, *refs[count + 9 :])
        split = EARLY * 2 * HALF

        def result(v, staged, slot):
            return pltpu.make_async_copy(staged, out_ref.at[v], out_sems.at[slot])

        def lags(i, carry):
            for slot, staged in ((0, staged0), (1, staged1)):
                v = 2 * i + slot

                @pl.when(i > 0)
                def _():
                    result(v - 2, staged, slot).wait()

                total = dot(table_ref[:, :split], early_ref[v]) + dot(table_ref[:, split:], crossed[v])
                staged[...] = total.astype(jnp.bfloat16)
                result(v, staged, slot).start()
            return carry

        lax.fori_loop(0, SOURCES // 2, lags, 0)
        result(SOURCES - 2, staged0, 0).wait()
        result(SOURCES - 1, staged1, 1).wait()

    return pl.pallas_call(
        kernel,
        out_shape=jax.ShapeDtypeStruct((SOURCES, LAGS, BLOCK), jnp.bfloat16),
        in_specs=[pl.BlockSpec(memory_space=pl.ANY)] * count + [pl.BlockSpec(memory_space=pltpu.VMEM)] * 4,
        out_specs=pl.BlockSpec(memory_space=pl.ANY),
        scratch_shapes=[
            pltpu.VMEM((SOURCES, late * 2 * HALF, BLOCK), jnp.bfloat16),
            pltpu.VMEM((LAGS, BLOCK), jnp.bfloat16),
            pltpu.VMEM((LAGS, BLOCK), jnp.bfloat16),
            pltpu.SemaphoreType.DMA((2,)),
            *cross_scratch(late),
        ],
        compiler_params=pltpu.CompilerParams(vmem_limit_bytes=26 * MIB),
        cost_estimate=pl.CostEstimate(flops=5 * 10**9, bytes_accessed=5 * MIB, transcendentals=0),
    )(*pieces, early, scale, white, table)


def table_kernel(col_ref, out_ref):
    col = col_ref[0]
    lane = lax.broadcasted_iota(jnp.int32, (1, 2 * FREQ), 1)
    freq = lane % HALF
    for g, (dx, dz, dc, half) in enumerate(GROUPS):
        base = place(col, dx, dz, dc) * 2 * HALF + half * HALF
        freq = freq + jnp.where(lane // (2 * HALF) == g, base, 0)
    shift = lane // HALF % 2 * (FREQ // 2)
    step = lax.broadcasted_iota(jnp.int32, (HALF, 2 * FREQ), 0)
    cosine = lambda phase: jnp.cos((phase % (2 * FREQ)).astype(jnp.float32) * (math.pi / FREQ))
    coarse, fine = HALF * step * freq + shift, step * freq
    quarter = 3 * FREQ // 2
    weight = jnp.where(freq == 0, 0.5, 1.0).astype(jnp.float32) / math.sqrt(2.0 * FREQ)
    cos0, sin0 = weight * cosine(coarse), weight * cosine(coarse + quarter)
    cos1, sin1 = cosine(fine), cosine(fine + quarter)
    for i in range(HALF):
        value = cos0[i : i + 1] * cos1 - sin0[i : i + 1] * sin1
        out_ref[i * HALF : (i + 1) * HALF, :] = value.astype(jnp.bfloat16)


def lag_table(col):
    return pl.pallas_call(
        table_kernel,
        out_shape=jax.ShapeDtypeStruct((LAGS, 2 * FREQ), jnp.bfloat16),
        in_specs=[pl.BlockSpec(memory_space=pltpu.SMEM)],
        compiler_params=pltpu.CompilerParams(vmem_limit_bytes=8 * MIB),
        cost_estimate=pl.CostEstimate(flops=10**6, bytes_accessed=10**4, transcendentals=0),
    )(col)


def send(value, axis, where):
    return lax.ppermute(value, axis, [(n, where(n)) for n in range(16)])


def on_slow(n, d):
    return (n // 4 + d) % 4 * 4 + n % 4


def spread(value, axis, groups):
    copies = jnp.broadcast_to(value[None], (len(groups[0]), *value.shape))
    return lax.all_to_all(copies, axis, 0, 0, tiled=True, axis_index_groups=groups)


def on_device(x, mask, pairing):
    col = lax.axis_index("col")
    up = lambda v: send(v, "col", lambda n: on_slow(n, 1))
    down = lambda v: send(v, "col", lambda n: on_slow(n, -1))
    across = lambda v: send(v, "col", lambda n: n ^ 2)
    sibling = lambda v: send(v, "col", lambda n: n ^ 1)
    low = lambda v: v[:, :, :HALF]
    high = lambda v: v[:, :, HALF:]
    join = lambda a, b: jnp.concatenate([a, b], axis=2)

    a1, b1, c1 = up(x), down(x), across(x)

    own, partial, good = prepare(x, mask.reshape(1, BLOCK))
    by_slow = jnp.stack([own] + [send(own, "row", lambda n, d=d: on_slow(n, d)) for d in (1, 2, 3)])
    by_row = spread(by_slow, "row", [[4 * a + b for b in range(4)] for a in range(4)])
    a2, b2, c2 = up(join(low(a1), high(c1))), down(join(low(c1), high(b1))), across(join(low(a1), high(b1)))
    a3, b3 = up(high(a2)), down(low(b2))
    chosen = choose(lax.axis_index("row").reshape(1), pairing, by_row, partial)
    chosen, table = lax.optimization_barrier((chosen, lag_table(col.reshape(1))))
    got = lax.all_to_all(chosen, "col", 0, 0, tiled=True)
    scale, white = scales(col.reshape(1), got, good)

    pair = lambda *mine: [piece for one in mine for piece in (one, sibling(one))]
    early = cross(pair(x, a1, b1, c1, a2, b2, c2), scale, white)
    early, a3, b3 = lax.optimization_barrier((early, a3, b3))
    return finish(pair(a3, b3), early, scale, white, table)


def solution(mesh):
    in_specs = (P(None, None, "col", "row"), P("row"), P("row", None))
    out_specs = P("col", None, "row")
    return jax.shard_map(on_device, mesh=mesh, in_specs=in_specs, out_specs=out_specs, check_vma=False)
```

```python
import math

import jax
import jax.numpy as jnp
import numpy as np
from jax import lax
from jax.experimental import pallas as pl
from jax.experimental.pallas import tpu as pltpu
from jax.sharding import PartitionSpec as P

BLOCK = 512
FREQ = 512
LAGS = 256
SEG = 8
SOURCES = 16
HALF = 16
STEP = BLOCK // SOURCES
GROUP = 2 * SEG * HALF
EPS = 1e-06
MIB = 1 << 20

BATCHES = (
    (
        ((0, 0, 0), (0, 0, 1)),
        ((1, 0, 0), (1, 0, 1)),
        ((3, 0, 0), (3, 0, 1)),
        ((0, 1, 0), (0, 1, 1)),
    ),
    (
        ((2, 0, 0), (1, 1, 1)),
        ((3, 1, 0), (2, 0, 1)),
        ((1, 1, 0), (3, 1, 1)),
    ),
    (((2, 1, 1),), ((2, 1, 0),)),
)


def ordered_groups(batch):
    return [(dx, dz, dc, half) for piece in batch for dc in (0, 1) for dx, dz, half in piece]


GROUPS = [group for batch in BATCHES for group in ordered_groups(batch)]

EARLY = sum(len(ordered_groups(batch)) for batch in BATCHES[:2])


def dot(a, b, dims=((1,), (0,))):
    return lax.dot_general(a, b, (dims, ((), ())), preferred_element_type=jnp.float32)


def place(col, dx, dz, dc):
    x, z, core = col // 4, col // 2 % 2, col % 2
    return (x + 4 - dx) % 4 * 4 + (z + dz) % 2 * 2 + (core + dc) % 2


def prepare_kernel(x_ref, mask_ref, src_ref, energy_ref, good_ref):
    mask = mask_ref[...].astype(jnp.float32)
    good_ref[...] = mask
    row = lax.broadcasted_iota(jnp.int32, (SOURCES, BLOCK), 0)
    col = lax.broadcasted_iota(jnp.int32, (SOURCES, BLOCK), 1)
    pick = jnp.where(col == row * STEP, jnp.broadcast_to(mask, (SOURCES, BLOCK)), 0.0).astype(jnp.bfloat16)
    for half in range(2):
        part = x_ref[:, :, half * HALF : (half + 1) * HALF, :].reshape(GROUP, BLOCK)
        src_ref[:, half * GROUP : (half + 1) * GROUP] = dot(pick, part, ((1,), (1,))).astype(jnp.bfloat16)
    sums = []
    for seg in range(SEG):
        value = x_ref[seg].astype(jnp.float32).reshape(4 * HALF, BLOCK)
        sums.append(jnp.sum(value * value, axis=0, keepdims=True))
    energy = jnp.concatenate(sums, axis=0) * mask
    high = energy.astype(jnp.bfloat16).astype(jnp.float32)
    energy_ref[...] = jnp.concatenate([high, energy - high], axis=0).astype(jnp.bfloat16)


def prepare(x, mask):
    return pl.pallas_call(
        prepare_kernel,
        out_shape=(jax.ShapeDtypeStruct((SOURCES, BLOCK), jnp.bfloat16),) * 2
        + (jax.ShapeDtypeStruct((1, BLOCK), jnp.float32),),
        compiler_params=pltpu.CompilerParams(vmem_limit_bytes=16 * MIB),
    )(x, mask)


def choose_kernel(row_ref, pairing_ref, gathered_ref, energy_ref, out_ref):
    row = row_ref[0]
    for slot in range(16):
        block = pairing_ref[0, slot]
        out_ref[slot, :SOURCES] = gathered_ref[block % 4, (row // 4 + 4 - block // 4) % 4]
        out_ref[slot, SOURCES:] = energy_ref[...]


def choose(row, pairing, gathered, energy):
    return pl.pallas_call(
        choose_kernel,
        out_shape=jax.ShapeDtypeStruct((16, 2 * SOURCES, BLOCK), jnp.bfloat16),
        in_specs=[pl.BlockSpec(memory_space=pltpu.SMEM)] * 2 + [pl.BlockSpec(memory_space=pltpu.VMEM)] * 2,
        compiler_params=pltpu.CompilerParams(vmem_limit_bytes=8 * MIB),
    )(row, pairing, gathered, energy)


def scales_kernel(col_ref, got_ref, good_ref, scale_ref, white_ref):
    energy = jnp.zeros((SEG, BLOCK), jnp.float32)
    for n in range(16):
        both = got_ref[n, SOURCES:].astype(jnp.float32)
        energy = energy + (both[:SEG] + both[SEG:])
    scale_ref[...] = good_ref[...] * lax.rsqrt(energy / FREQ + EPS)

    power = jnp.zeros((SOURCES, 2 * GROUP), jnp.float32)
    for n in range(16):
        value = got_ref[n, :SOURCES].astype(jnp.float32)
        power = power + value * value
    power = power[:, :GROUP] + power[:, GROUP:]
    row = lax.broadcasted_iota(jnp.int32, (GROUP, GROUP), 0)
    col = lax.broadcasted_iota(jnp.int32, (GROUP, GROUP), 1)
    same = jnp.where(row // (2 * HALF) == col // (2 * HALF), 1.0, 0.0)
    total = lax.dot_general(
        power, same, (((1,), (0,)), ((), ())), precision=lax.Precision.HIGHEST, preferred_element_type=jnp.float32
    )
    factor = lax.rsqrt(total / FREQ + EPS)
    turn = jnp.where(row == col + HALF, 1.0, 0.0) - jnp.where(row == col - HALF, 1.0, 0.0)
    first = (col // HALF) % 2 == 0
    turn = jnp.where(first, jnp.maximum(turn, 0.0), jnp.minimum(turn, 0.0)).astype(jnp.bfloat16)
    for g, (dx, dz, dc, half) in enumerate(GROUPS):
        n = place(col_ref[0], dx, dz, dc)
        value = got_ref[n, :SOURCES, half * GROUP : (half + 1) * GROUP].astype(jnp.float32)
        real = (value * factor).astype(jnp.bfloat16)
        white_ref[g, :SOURCES] = real
        white_ref[g, SOURCES:] = dot(real, turn).astype(jnp.bfloat16)


def cross_groups(pieces, first_group, scale_ref, white_ref, crossed, raw, right0, right1, left0, left1, sems, setup=None):
    copies = []
    for piece in pieces:
        for half in range(piece.shape[2] // HALF):
            g = len(copies)
            copies.append(pltpu.make_async_copy(piece.at[:, :, pl.ds(half * HALF, HALF), :], raw.at[g], sems.at[g]))
    for copy in copies:
        copy.start()
    groups = len(copies)
    if setup is not None:
        setup()

    def arrive(g):
        pltpu.make_async_copy(raw.at[g], raw.at[g], sems.at[g]).wait()

    lane = lax.broadcasted_iota(jnp.int32, (HALF, GROUP), 1)
    sub = lax.broadcasted_iota(jnp.int32, (HALF, GROUP), 0)
    diagonal = lane % HALF == sub

    def ready(g, right, left):
        for seg in range(SEG):
            value = raw[g, seg].astype(jnp.float32) * scale_ref[seg : seg + 1, :].reshape(1, 1, BLOCK)
            right[seg * 2 * HALF : (seg + 1) * 2 * HALF, :] = value.astype(jnp.bfloat16).reshape(2 * HALF, BLOCK)
        white = white_ref[first_group + g].astype(jnp.float32)
        for v in range(SOURCES):
            for part in range(2):
                one = white[part * SOURCES + v : part * SOURCES + v + 1, :]
                tile = jnp.where(diagonal, jnp.broadcast_to(one, (HALF, GROUP)), 0.0).astype(jnp.bfloat16)
                left[(2 * v + part) * HALF : (2 * v + part + 1) * HALF, :] = tile

    def multiply(g, right, left):
        rows = pl.ds(pl.multiple_of(g * 2 * HALF, 2 * HALF), 2 * HALF)
        for n in range(0, BLOCK, GROUP):
            value = dot(left[...], right[:, n : n + GROUP]).astype(jnp.bfloat16)
            crossed[:, rows, n : n + GROUP] = value.reshape(SOURCES, 2 * HALF, GROUP)

    arrive(0)
    ready(0, right0, left0)

    def pair(i, carry):
        g = 2 * i
        arrive(g + 1)
        multiply(g, right0, left0)
        ready(g + 1, right1, left1)

        @pl.when(i < groups // 2 - 1)
        def _():
            arrive(g + 2)

        multiply(g + 1, right1, left1)
        ready(jnp.minimum(g + 2, groups - 1), right0, left0)
        return carry

    lax.fori_loop(0, groups // 2, pair, 0)


def cross_scratch(groups):
    return [
        pltpu.VMEM((groups, SEG, 2, HALF, BLOCK), jnp.bfloat16),
        pltpu.VMEM((GROUP, BLOCK), jnp.bfloat16),
        pltpu.VMEM((GROUP, BLOCK), jnp.bfloat16),
        pltpu.VMEM((2 * SOURCES * HALF, GROUP), jnp.bfloat16),
        pltpu.VMEM((2 * SOURCES * HALF, GROUP), jnp.bfloat16),
        pltpu.SemaphoreType.DMA((groups,)),
    ]


def cross(pieces, col, got, good):
    count = len(pieces)

    def kernel(*refs):
        col_ref, got_ref, good_ref, out_ref, scale_ref, white_ref = refs[count : count + 6]
        setup = lambda: scales_kernel(col_ref, got_ref, good_ref, scale_ref, white_ref)
        cross_groups(refs[:count], 0, scale_ref, white_ref, out_ref, *refs[count + 6 :], setup=setup)

    return pl.pallas_call(
        kernel,
        out_shape=(
            jax.ShapeDtypeStruct((SOURCES, EARLY * 2 * HALF, BLOCK), jnp.bfloat16),
            jax.ShapeDtypeStruct((SEG, BLOCK), jnp.float32),
            jax.ShapeDtypeStruct((len(GROUPS), 2 * SOURCES, GROUP), jnp.bfloat16),
        ),
        in_specs=[pl.BlockSpec(memory_space=pl.ANY)] * count
        + [pl.BlockSpec(memory_space=pltpu.SMEM)]
        + [pl.BlockSpec(memory_space=pltpu.VMEM)] * 2,
        scratch_shapes=cross_scratch(EARLY),
        compiler_params=pltpu.CompilerParams(vmem_limit_bytes=16 * MIB),
        cost_estimate=pl.CostEstimate(flops=10**9, bytes_accessed=MIB, transcendentals=0),
    )(*pieces, col, got, good)


def finish(pieces, early, scale, white, table):
    count, late = len(pieces), len(GROUPS) - EARLY

    def kernel(*refs):
        early_ref, scale_ref, white_ref, table_ref, out_ref, crossed, staged0, staged1, out_sems = refs[count : count + 9]
        cross_groups(refs[:count], EARLY, scale_ref, white_ref, crossed, *refs[count + 9 :])
        split = EARLY * 2 * HALF

        def result(v, staged, slot):
            return pltpu.make_async_copy(staged, out_ref.at[v], out_sems.at[slot])

        def lags(i, carry):
            for slot, staged in ((0, staged0), (1, staged1)):
                v = 2 * i + slot

                @pl.when(i > 0)
                def _():
                    result(v - 2, staged, slot).wait()

                total = dot(table_ref[:, :split], early_ref[v]) + dot(table_ref[:, split:], crossed[v])
                staged[...] = total.astype(jnp.bfloat16)
                result(v, staged, slot).start()
            return carry

        lax.fori_loop(0, SOURCES // 2, lags, 0)
        result(SOURCES - 2, staged0, 0).wait()
        result(SOURCES - 1, staged1, 1).wait()

    return pl.pallas_call(
        kernel,
        out_shape=jax.ShapeDtypeStruct((SOURCES, LAGS, BLOCK), jnp.bfloat16),
        in_specs=[pl.BlockSpec(memory_space=pl.ANY)] * count + [pl.BlockSpec(memory_space=pltpu.VMEM)] * 4,
        out_specs=pl.BlockSpec(memory_space=pl.ANY),
        scratch_shapes=[
            pltpu.VMEM((SOURCES, late * 2 * HALF, BLOCK), jnp.bfloat16),
            pltpu.VMEM((LAGS, BLOCK), jnp.bfloat16),
            pltpu.VMEM((LAGS, BLOCK), jnp.bfloat16),
            pltpu.SemaphoreType.DMA((2,)),
            *cross_scratch(late),
        ],
        compiler_params=pltpu.CompilerParams(vmem_limit_bytes=12 * MIB),
        cost_estimate=pl.CostEstimate(flops=5 * 10**9, bytes_accessed=5 * MIB, transcendentals=0),
    )(*pieces, early, scale, white, table)


def table_kernel(col_ref, out_ref):
    col = col_ref[0]
    lane = lax.broadcasted_iota(jnp.int32, (1, 2 * FREQ), 1)
    freq = lane % HALF
    for g, (dx, dz, dc, half) in enumerate(GROUPS):
        base = place(col, dx, dz, dc) * 2 * HALF + half * HALF
        freq = freq + jnp.where(lane // (2 * HALF) == g, base, 0)
    shift = lane // HALF % 2 * (FREQ // 2)
    step = lax.broadcasted_iota(jnp.int32, (HALF, 2 * FREQ), 0)
    cosine = lambda phase: jnp.cos((phase % (2 * FREQ)).astype(jnp.float32) * (math.pi / FREQ))
    coarse, fine = HALF * step * freq + shift, step * freq
    quarter = 3 * FREQ // 2
    weight = jnp.where(freq == 0, 0.5, 1.0).astype(jnp.float32) / math.sqrt(2.0 * FREQ)
    cos0, sin0 = weight * cosine(coarse), weight * cosine(coarse + quarter)
    cos1, sin1 = cosine(fine), cosine(fine + quarter)
    for i in range(HALF):
        value = cos0[i : i + 1] * cos1 - sin0[i : i + 1] * sin1
        out_ref[i * HALF : (i + 1) * HALF, :] = value.astype(jnp.bfloat16)


def lag_table(col):
    return pl.pallas_call(
        table_kernel,
        out_shape=jax.ShapeDtypeStruct((LAGS, 2 * FREQ), jnp.bfloat16),
        in_specs=[pl.BlockSpec(memory_space=pltpu.SMEM)],
        compiler_params=pltpu.CompilerParams(vmem_limit_bytes=8 * MIB),
        cost_estimate=pl.CostEstimate(flops=10**6, bytes_accessed=10**4, transcendentals=0),
    )(col)


def send(value, axis, where):
    return lax.ppermute(value, axis, [(n, where(n)) for n in range(16)])


def on_slow(n, d):
    return (n // 4 + d) % 4 * 4 + n % 4


def spread(value, axis, groups):
    copies = jnp.broadcast_to(value[None], (len(groups[0]), *value.shape))
    return lax.all_to_all(copies, axis, 0, 0, tiled=True, axis_index_groups=groups)


def on_device(x, mask, pairing):
    col = lax.axis_index("col")
    up = lambda v: send(v, "col", lambda n: on_slow(n, 1))
    down = lambda v: send(v, "col", lambda n: on_slow(n, -1))
    across = lambda v: send(v, "col", lambda n: n ^ 2)
    sibling = lambda v: send(v, "col", lambda n: n ^ 1)
    low = lambda v: v[:, :, :HALF]
    high = lambda v: v[:, :, HALF:]
    join = lambda a, b: jnp.concatenate([a, b], axis=2)

    a1, b1, c1 = up(x), down(x), across(x)

    own, partial, good = prepare(x, mask.reshape(1, BLOCK))
    by_slow = jnp.stack([own] + [send(own, "row", lambda n, d=d: on_slow(n, d)) for d in (1, 2, 3)])
    by_row = spread(by_slow, "row", [[4 * a + b for b in range(4)] for a in range(4)])
    a2, b2, c2 = up(join(low(a1), high(c1))), down(join(low(c1), high(b1))), across(join(low(a1), high(b1)))
    a3, b3 = up(high(a2)), down(low(b2))
    chosen = choose(lax.axis_index("row").reshape(1), pairing, by_row, partial)
    chosen, table = lax.optimization_barrier((chosen, lag_table(col.reshape(1))))
    got = lax.all_to_all(chosen, "col", 0, 0, tiled=True)

    pair = lambda *mine: [piece for one in mine for piece in (one, sibling(one))]
    early, scale, white = cross(pair(x, a1, b1, c1, a2, b2, c2), col.reshape(1), got, good)
    early, a3, b3 = lax.optimization_barrier((early, a3, b3))
    return finish(pair(a3, b3), early, scale, white, table)


def solution(mesh):
    in_specs = (P(None, None, "col", "row"), P("row"), P("row", None))
    out_specs = P("col", None, "row")
    return jax.shard_map(on_device, mesh=mesh, in_specs=in_specs, out_specs=out_specs, check_vma=False)
```

```python
import math

import jax
import jax.numpy as jnp
import numpy as np
from jax import lax
from jax.experimental import pallas as pl
from jax.experimental.pallas import tpu as pltpu
from jax.sharding import PartitionSpec as P

BLOCK = 512
FREQ = 512
LAGS = 256
SEG = 8
SOURCES = 16
HALF = 16
STEP = BLOCK // SOURCES
GROUP = 2 * SEG * HALF
EPS = 1e-06
MIB = 1 << 20

BATCHES = (
    (
        ((0, 0, 0), (0, 0, 1)),
        ((1, 0, 0), (1, 0, 1)),
        ((3, 0, 0), (3, 0, 1)),
        ((0, 1, 0), (0, 1, 1)),
    ),
    (
        ((2, 0, 0), (1, 1, 1)),
        ((3, 1, 0), (2, 0, 1)),
        ((1, 1, 0), (3, 1, 1)),
    ),
    (((2, 1, 1),), ((2, 1, 0),)),
)


def ordered_groups(batch):
    return [(dx, dz, dc, half) for piece in batch for dc in (0, 1) for dx, dz, half in piece]


GROUPS = [group for batch in BATCHES for group in ordered_groups(batch)]

EARLY = sum(len(ordered_groups(batch)) for batch in BATCHES[:2])


def dot(a, b, dims=((1,), (0,))):
    return lax.dot_general(a, b, (dims, ((), ())), preferred_element_type=jnp.float32)


def place(col, dx, dz, dc):
    x, z, core = col // 4, col // 2 % 2, col % 2
    return (x + 4 - dx) % 4 * 4 + (z + dz) % 2 * 2 + (core + dc) % 2


def prepare_kernel(x_ref, mask_ref, src_ref, energy_ref, good_ref, near, sem):
    copy = pltpu.make_async_copy(mask_ref, near, sem)
    copy.start()
    sums = []
    for seg in range(SEG):
        value = x_ref[seg].astype(jnp.float32).reshape(4 * HALF, BLOCK)
        sums.append(jnp.sum(value * value, axis=0, keepdims=True))
    copy.wait()
    mask = near[...].astype(jnp.float32)
    good_ref[...] = mask
    row = lax.broadcasted_iota(jnp.int32, (SOURCES, BLOCK), 0)
    col = lax.broadcasted_iota(jnp.int32, (SOURCES, BLOCK), 1)
    pick = jnp.where(col == row * STEP, jnp.broadcast_to(mask, (SOURCES, BLOCK)), 0.0).astype(jnp.bfloat16)
    for half in range(2):
        part = x_ref[:, :, half * HALF : (half + 1) * HALF, :].reshape(GROUP, BLOCK)
        src_ref[:, half * GROUP : (half + 1) * GROUP] = dot(pick, part, ((1,), (1,))).astype(jnp.bfloat16)
    energy = jnp.concatenate(sums, axis=0) * mask
    high = energy.astype(jnp.bfloat16).astype(jnp.float32)
    energy_ref[...] = jnp.concatenate([high, energy - high], axis=0).astype(jnp.bfloat16)


def prepare(x, mask):
    return pl.pallas_call(
        prepare_kernel,
        out_shape=(jax.ShapeDtypeStruct((SOURCES, BLOCK), jnp.bfloat16),) * 2
        + (jax.ShapeDtypeStruct((1, BLOCK), jnp.float32),),
        in_specs=[pl.BlockSpec(memory_space=pltpu.VMEM), pl.BlockSpec(memory_space=pl.ANY)],
        scratch_shapes=[pltpu.VMEM((1, BLOCK), jnp.int32), pltpu.SemaphoreType.DMA],
        compiler_params=pltpu.CompilerParams(vmem_limit_bytes=16 * MIB),
    )(x, mask)


def choose_kernel(row_ref, pairing_ref, gathered_ref, energy_ref, out_ref, near, sem):
    copy = pltpu.make_async_copy(pairing_ref, near, sem)
    copy.start()
    for slot in range(16):
        out_ref[slot, SOURCES:] = energy_ref[...]
    copy.wait()
    row = row_ref[0]
    for slot in range(16):
        block = near[0, slot]
        out_ref[slot, :SOURCES] = gathered_ref[block % 4, (row // 4 + 4 - block // 4) % 4]


def choose(row, pairing, gathered, energy):
    return pl.pallas_call(
        choose_kernel,
        out_shape=jax.ShapeDtypeStruct((16, 2 * SOURCES, BLOCK), jnp.bfloat16),
        in_specs=[pl.BlockSpec(memory_space=pltpu.SMEM), pl.BlockSpec(memory_space=pl.ANY)]
        + [pl.BlockSpec(memory_space=pltpu.VMEM)] * 2,
        scratch_shapes=[pltpu.SMEM((1, 16), jnp.int32), pltpu.SemaphoreType.DMA],
        compiler_params=pltpu.CompilerParams(vmem_limit_bytes=8 * MIB),
    )(row, pairing, gathered, energy)


def scales_kernel(col_ref, got_ref, good_ref, scale_ref, white_ref):
    energy = jnp.zeros((SEG, BLOCK), jnp.float32)
    for n in range(16):
        both = got_ref[n, SOURCES:].astype(jnp.float32)
        energy = energy + (both[:SEG] + both[SEG:])
    scale_ref[...] = good_ref[...] * lax.rsqrt(energy / FREQ + EPS)

    power = jnp.zeros((SOURCES, 2 * GROUP), jnp.float32)
    for n in range(16):
        value = got_ref[n, :SOURCES].astype(jnp.float32)
        power = power + value * value
    power = power[:, :GROUP] + power[:, GROUP:]
    row = lax.broadcasted_iota(jnp.int32, (GROUP, GROUP), 0)
    col = lax.broadcasted_iota(jnp.int32, (GROUP, GROUP), 1)
    same = jnp.where(row // (2 * HALF) == col // (2 * HALF), 1.0, 0.0)
    total = lax.dot_general(
        power, same, (((1,), (0,)), ((), ())), precision=lax.Precision.HIGHEST, preferred_element_type=jnp.float32
    )
    factor = lax.rsqrt(total / FREQ + EPS)
    turn = jnp.where(row == col + HALF, 1.0, 0.0) - jnp.where(row == col - HALF, 1.0, 0.0)
    first = (col // HALF) % 2 == 0
    turn = jnp.where(first, jnp.maximum(turn, 0.0), jnp.minimum(turn, 0.0)).astype(jnp.bfloat16)
    for g, (dx, dz, dc, half) in enumerate(GROUPS):
        n = place(col_ref[0], dx, dz, dc)
        value = got_ref[n, :SOURCES, half * GROUP : (half + 1) * GROUP].astype(jnp.float32)
        real = (value * factor).astype(jnp.bfloat16)
        white_ref[g, :SOURCES] = real
        white_ref[g, SOURCES:] = dot(real, turn).astype(jnp.bfloat16)


def cross_groups(pieces, first_group, scale_ref, white_ref, crossed, raw, right0, right1, left0, left1, sems, setup=None):
    copies = []
    for piece in pieces:
        for half in range(piece.shape[2] // HALF):
            g = len(copies)
            copies.append(pltpu.make_async_copy(piece.at[:, :, pl.ds(half * HALF, HALF), :], raw.at[g], sems.at[g]))
    for copy in copies:
        copy.start()
    groups = len(copies)
    if setup is not None:
        setup()

    def arrive(g):
        pltpu.make_async_copy(raw.at[g], raw.at[g], sems.at[g]).wait()

    lane = lax.broadcasted_iota(jnp.int32, (HALF, GROUP), 1)
    sub = lax.broadcasted_iota(jnp.int32, (HALF, GROUP), 0)
    diagonal = lane % HALF == sub

    def ready(g, right, left):
        for seg in range(SEG):
            value = raw[g, seg].astype(jnp.float32) * scale_ref[seg : seg + 1, :].reshape(1, 1, BLOCK)
            right[seg * 2 * HALF : (seg + 1) * 2 * HALF, :] = value.astype(jnp.bfloat16).reshape(2 * HALF, BLOCK)
        white = white_ref[first_group + g].astype(jnp.float32)
        for v in range(SOURCES):
            for part in range(2):
                one = white[part * SOURCES + v : part * SOURCES + v + 1, :]
                tile = jnp.where(diagonal, jnp.broadcast_to(one, (HALF, GROUP)), 0.0).astype(jnp.bfloat16)
                left[(2 * v + part) * HALF : (2 * v + part + 1) * HALF, :] = tile

    def multiply(g, right, left):
        rows = pl.ds(pl.multiple_of(g * 2 * HALF, 2 * HALF), 2 * HALF)
        for n in range(0, BLOCK, GROUP):
            value = dot(left[...], right[:, n : n + GROUP]).astype(jnp.bfloat16)
            crossed[:, rows, n : n + GROUP] = value.reshape(SOURCES, 2 * HALF, GROUP)

    arrive(0)
    ready(0, right0, left0)

    def pair(i, carry):
        g = 2 * i
        arrive(g + 1)
        multiply(g, right0, left0)
        ready(g + 1, right1, left1)

        @pl.when(i < groups // 2 - 1)
        def _():
            arrive(g + 2)

        multiply(g + 1, right1, left1)
        ready(jnp.minimum(g + 2, groups - 1), right0, left0)
        return carry

    lax.fori_loop(0, groups // 2, pair, 0)


def cross_scratch(groups):
    return [
        pltpu.VMEM((groups, SEG, 2, HALF, BLOCK), jnp.bfloat16),
        pltpu.VMEM((GROUP, BLOCK), jnp.bfloat16),
        pltpu.VMEM((GROUP, BLOCK), jnp.bfloat16),
        pltpu.VMEM((2 * SOURCES * HALF, GROUP), jnp.bfloat16),
        pltpu.VMEM((2 * SOURCES * HALF, GROUP), jnp.bfloat16),
        pltpu.SemaphoreType.DMA((groups,)),
    ]


def cross(pieces, col, got, good):
    count = len(pieces)

    def kernel(*refs):
        col_ref, got_ref, good_ref, out_ref, scale_ref, white_ref = refs[count : count + 6]
        setup = lambda: scales_kernel(col_ref, got_ref, good_ref, scale_ref, white_ref)
        cross_groups(refs[:count], 0, scale_ref, white_ref, out_ref, *refs[count + 6 :], setup=setup)

    return pl.pallas_call(
        kernel,
        out_shape=(
            jax.ShapeDtypeStruct((SOURCES, EARLY * 2 * HALF, BLOCK), jnp.bfloat16),
            jax.ShapeDtypeStruct((SEG, BLOCK), jnp.float32),
            jax.ShapeDtypeStruct((len(GROUPS), 2 * SOURCES, GROUP), jnp.bfloat16),
        ),
        in_specs=[pl.BlockSpec(memory_space=pl.ANY)] * count
        + [pl.BlockSpec(memory_space=pltpu.SMEM)]
        + [pl.BlockSpec(memory_space=pltpu.VMEM)] * 2,
        scratch_shapes=cross_scratch(EARLY),
        compiler_params=pltpu.CompilerParams(vmem_limit_bytes=16 * MIB),
        cost_estimate=pl.CostEstimate(flops=10**9, bytes_accessed=MIB, transcendentals=0),
    )(*pieces, col, got, good)


def finish(pieces, early, scale, white, table):
    count, late = len(pieces), len(GROUPS) - EARLY

    def kernel(*refs):
        early_ref, scale_ref, white_ref, table_ref, out_ref, crossed, staged0, staged1, out_sems = refs[count : count + 9]
        cross_groups(refs[:count], EARLY, scale_ref, white_ref, crossed, *refs[count + 9 :])
        split = EARLY * 2 * HALF

        def result(v, staged, slot):
            return pltpu.make_async_copy(staged, out_ref.at[v], out_sems.at[slot])

        def lags(i, carry):
            for slot, staged in ((0, staged0), (1, staged1)):
                v = 2 * i + slot

                @pl.when(i > 0)
                def _():
                    result(v - 2, staged, slot).wait()

                total = dot(table_ref[:, :split], early_ref[v]) + dot(table_ref[:, split:], crossed[v])
                staged[...] = total.astype(jnp.bfloat16)
                result(v, staged, slot).start()
            return carry

        lax.fori_loop(0, SOURCES // 2, lags, 0)
        result(SOURCES - 2, staged0, 0).wait()
        result(SOURCES - 1, staged1, 1).wait()

    return pl.pallas_call(
        kernel,
        out_shape=jax.ShapeDtypeStruct((SOURCES, LAGS, BLOCK), jnp.bfloat16),
        in_specs=[pl.BlockSpec(memory_space=pl.ANY)] * count + [pl.BlockSpec(memory_space=pltpu.VMEM)] * 4,
        out_specs=pl.BlockSpec(memory_space=pl.ANY),
        scratch_shapes=[
            pltpu.VMEM((SOURCES, late * 2 * HALF, BLOCK), jnp.bfloat16),
            pltpu.VMEM((LAGS, BLOCK), jnp.bfloat16),
            pltpu.VMEM((LAGS, BLOCK), jnp.bfloat16),
            pltpu.SemaphoreType.DMA((2,)),
            *cross_scratch(late),
        ],
        compiler_params=pltpu.CompilerParams(vmem_limit_bytes=12 * MIB),
        cost_estimate=pl.CostEstimate(flops=5 * 10**9, bytes_accessed=5 * MIB, transcendentals=0),
    )(*pieces, early, scale, white, table)


def table_kernel(col_ref, out_ref):
    col = col_ref[0]
    lane = lax.broadcasted_iota(jnp.int32, (1, 2 * FREQ), 1)
    freq = lane % HALF
    for g, (dx, dz, dc, half) in enumerate(GROUPS):
        base = place(col, dx, dz, dc) * 2 * HALF + half * HALF
        freq = freq + jnp.where(lane // (2 * HALF) == g, base, 0)
    shift = lane // HALF % 2 * (FREQ // 2)
    step = lax.broadcasted_iota(jnp.int32, (HALF, 2 * FREQ), 0)
    cosine = lambda phase: jnp.cos((phase % (2 * FREQ)).astype(jnp.float32) * (math.pi / FREQ))
    coarse, fine = HALF * step * freq + shift, step * freq
    quarter = 3 * FREQ // 2
    weight = jnp.where(freq == 0, 0.5, 1.0).astype(jnp.float32) / math.sqrt(2.0 * FREQ)
    cos0, sin0 = weight * cosine(coarse), weight * cosine(coarse + quarter)
    cos1, sin1 = cosine(fine), cosine(fine + quarter)
    for i in range(HALF):
        value = cos0[i : i + 1] * cos1 - sin0[i : i + 1] * sin1
        out_ref[i * HALF : (i + 1) * HALF, :] = value.astype(jnp.bfloat16)


def lag_table(col):
    return pl.pallas_call(
        table_kernel,
        out_shape=jax.ShapeDtypeStruct((LAGS, 2 * FREQ), jnp.bfloat16),
        in_specs=[pl.BlockSpec(memory_space=pltpu.SMEM)],
        compiler_params=pltpu.CompilerParams(vmem_limit_bytes=8 * MIB),
        cost_estimate=pl.CostEstimate(flops=10**6, bytes_accessed=10**4, transcendentals=0),
    )(col)


def send(value, axis, where):
    return lax.ppermute(value, axis, [(n, where(n)) for n in range(16)])


def on_slow(n, d):
    return (n // 4 + d) % 4 * 4 + n % 4


def spread(value, axis, groups):
    copies = jnp.broadcast_to(value[None], (len(groups[0]), *value.shape))
    return lax.all_to_all(copies, axis, 0, 0, tiled=True, axis_index_groups=groups)


def on_device(x, mask, pairing):
    col = lax.axis_index("col")
    up = lambda v: send(v, "col", lambda n: on_slow(n, 1))
    down = lambda v: send(v, "col", lambda n: on_slow(n, -1))
    across = lambda v: send(v, "col", lambda n: n ^ 2)
    sibling = lambda v: send(v, "col", lambda n: n ^ 1)
    low = lambda v: v[:, :, :HALF]
    high = lambda v: v[:, :, HALF:]
    join = lambda a, b: jnp.concatenate([a, b], axis=2)

    a1, b1, c1 = up(x), down(x), across(x)

    own, partial, good = prepare(x, mask.reshape(1, BLOCK))
    by_slow = jnp.stack([own] + [send(own, "row", lambda n, d=d: on_slow(n, d)) for d in (1, 2, 3)])
    by_row = spread(by_slow, "row", [[4 * a + b for b in range(4)] for a in range(4)])
    a2, b2, c2 = up(join(low(a1), high(c1))), down(join(low(c1), high(b1))), across(join(low(a1), high(b1)))
    a3, b3 = up(high(a2)), down(low(b2))
    chosen = choose(lax.axis_index("row").reshape(1), pairing, by_row, partial)
    chosen, table = lax.optimization_barrier((chosen, lag_table(col.reshape(1))))
    got = lax.all_to_all(chosen, "col", 0, 0, tiled=True)

    pair = lambda *mine: [piece for one in mine for piece in (one, sibling(one))]
    early, scale, white = cross(pair(x, a1, b1, c1, a2, b2, c2), col.reshape(1), got, good)
    early, a3, b3 = lax.optimization_barrier((early, a3, b3))
    return finish(pair(a3, b3), early, scale, white, table)


def solution(mesh):
    in_specs = (P(None, None, "col", "row"), P("row"), P("row", None))
    out_specs = P("col", None, "row")
    return jax.shard_map(on_device, mesh=mesh, in_specs=in_specs, out_specs=out_specs, check_vma=False)
```
